32 devices in a mesh: kv: 4 (over z), ep: 8 (over y, x, core).
Axes of the slice: x: 2, y: 2, z: 4, core: 2. Of those that a mesh axis runs over, the one named last changes fastest.
Arguments:
- queries: bfloat16 [8, 64, 2048], P('ep'), may hold values from -12 to 12
- new_keys: bfloat16 [8, 64, 512], P('ep'), may hold values from -12 to 12
- new_values: bfloat16 [8, 64, 512], P('ep'), may hold values from -6 to 6
- cache_keys: bfloat16 [8, 16, 128, 512], P('ep', 'kv'), may hold values from -12 to 12
- cache_values: bfloat16 [8, 16, 128, 512], P('ep', 'kv'), may hold values from -10 to 10
- page_table: int32 [8, 16], P('ep'), may hold values from 0 to 15, each once within a row
- cached_len: int32 [8], P('ep'), may hold values from 1 to 2048, 4096 in all
- moe_rows: bfloat16 [256, 4096], P('ep'), may hold values from -6 to 6
- expert_ids: int32 [256, 2], P('ep'), may hold values from 0 to 7, all different within a row; in each aligned block of 32 rows (0 to 31, 32 to 63, ...) at most 16 rows name the same one
- gate_probs: float32 [256, 2], P('ep'), may hold values from 0.1 to 0.9
- w_gate: bfloat16 [8, 4096, 8192], P('ep', None, 'kv'), may hold values from -0.09375 to 0.09375
- w_up: bfloat16 [8, 4096, 8192], P('ep', None, 'kv'), may hold values from -0.09375 to 0.09375
- w_down: bfloat16 [8, 8192, 4096], P('ep', 'kv'), may hold values from -0.09375 to 0.09375
Outputs:
- attn_out: bfloat16 [8, 64, 2048], P('ep')
- moe_out: bfloat16 [256, 4096], P('ep', 'kv')
The draws below stay inside these ranges and needn't reach their ends.
Inputs may be any that keep to these rules, and one draw needn't show every extreme that they name: `page_table`: each row is a permutation of the 16 slots of its request. `cached_len`: cached positions at or past a request's length hold no data. `expert_ids`: each row names 2 different experts; among the 32 rows of one ep index no expert is named more than 16 times, and this bound is reached.
All inputs are finite; a program needn't handle non-finite values. No bound on the sum of `cached_len` on one device may be relied on, other than what follows from the above.
Results may differ from the reference program's by a relative error of at most 0.0085.
Values may be sent and summed in bfloat16 or wider, within the bound.
A program may use at most 128 MiB of HBM per device.

```python
import math
import jax
import jax.numpy as jnp
import numpy as np
from jax import lax

D = 4096
HD = 128
EXPERTS = 8
TOP = 2
HQ = 16
KVH = 4
FF = 8192
PAGE = 128
NEW = 64
TOK_EP = 32
REQS = 8
POOL_COL = 16
MAXLEN = 2048
MTOK = 256
CAP = 16
GROUP = 1
FF_COL = 8192
N_EP = 8


def draw_queries(key, part):
    full_shape = (REQS, NEW, HQ, HD)
    drawn = jax.random.normal(key, full_shape, jnp.float32)
    return jnp.clip(drawn, -12.0, 12.0).reshape(REQS, NEW, HQ * HD).astype(jnp.bfloat16)


def draw_new_keys(key, part):
    full_shape = (REQS, NEW, KVH, HD)
    drawn = jax.random.normal(key, full_shape, jnp.float32)
    return jnp.clip(drawn, -12.0, 12.0).reshape(REQS, NEW, KVH * HD).astype(jnp.bfloat16)


def draw_cache_keys(key, part):
    full_shape = (REQS, POOL_COL, PAGE, KVH, HD)
    drawn = jnp.clip(jax.random.normal(key, full_shape, jnp.float32), -6.0, 6.0)
    return jnp.clip(drawn, -12.0, 12.0).reshape(REQS, POOL_COL, PAGE, KVH * HD).astype(jnp.bfloat16)


def draw_cache_values(key, part):
    noise_key, page_key = jax.random.split(key)
    full_shape = (REQS, POOL_COL, PAGE, KVH * HD)
    page_shape = (REQS, POOL_COL, 1, KVH * HD)
    drawn = jax.random.normal(noise_key, full_shape, jnp.float32)
    offsets = 1.5 * jax.random.normal(page_key, page_shape, jnp.float32)
    return jnp.clip(drawn + offsets, -10.0, 10.0).astype(jnp.bfloat16)


def with_spikes(array, stream_key, source, target, shards_of, factor):
    owner, partner = [(jnp.arange(array.shape[dim]) // (array.shape[dim] // shards_of)).reshape([-1 if axis == dim else 1 for axis in range(array.ndim)]) for dim in (source, target)]
    chosen = jax.random.permutation(stream_key, shards_of)[partner]
    strong = (owner == chosen) | (owner == (partner + shards_of // 2) % shards_of)
    return jnp.where(strong, factor * array, array)


def shard_levels(rng, dims, cuts, smallest, top_value):
    factor_of = 1.0
    for axis_at, shards_of in cuts:
        draws = jax.random.uniform(jax.random.fold_in(jax.random.fold_in(rng, 6), axis_at), (shards_of,), jnp.float32, smallest / len(cuts), top_value / len(cuts))
        factor_of = factor_of * jnp.repeat(jnp.exp(draws), dims[axis_at] // shards_of).reshape((-1,) + (1,) * (len(dims) - 1 - axis_at))
    return factor_of


def split_up(count, total, reach, slope):
    portions = [(1 << 20) // math.isqrt(standing ** slope) + 1 for standing in range(2, count + 1)]
    rest, holding = total - reach - (count - 1), [1] * (count - 1)
    while rest > 0:
        candidates = [i for i in range(count - 1) if holding[i] < reach]
        pool, left = sum([portions[i] for i in candidates]), rest
        for i in candidates:
            addition = min(reach - holding[i], max(1, left * portions[i] // pool), rest)
            holding[i] = holding[i] + addition
            rest = rest - addition
    return np.array([reach] + holding)


def ragged_sizes(stream_key, amount, total, most, slope):
    if amount == 2:
        one = jax.random.randint(stream_key, (), max(1, total - most), min(most, total - 1) + 1)
        return jnp.stack([one, total - one])
    tallies = jnp.asarray(split_up(amount, total, most, slope), jnp.int32)
    pairs = (amount - 1) // 2
    giver, sink = tallies[1:1 + 2 * pairs:2], tallies[2:2 + 2 * pairs:2]
    margin = jnp.minimum(giver - 1, most - sink)
    shifted = jax.random.randint(jax.random.fold_in(stream_key, 1), (pairs,), 0, 1 << 20) % (margin + 1)
    tallies = tallies.at[1:1 + 2 * pairs:2].set(giver - shifted).at[2:2 + 2 * pairs:2].set(sink + shifted)
    return tallies[jax.random.permutation(jax.random.fold_in(stream_key, 2), amount)]


def routed_block(own_key, own, number, rows, count, top, limit, lean):
    sequence = jax.random.permutation(own_key, count)
    heavy_load, common = portions_of(count, rows * top, limit, lean, True), portions_of(count, rows * top, limit, lean, False)
    places = jnp.arange(count)

    def named(tallies, offset_by):
        used = int((tallies > 0).sum())
        fixed = max(1, used // 4)
        passed = fixed + (places - fixed + offset_by * (used - fixed)) % max(1, count - fixed)
        return jnp.zeros((count,), jnp.int32).at[sequence[jnp.where(places < fixed, places, passed)]].set(jnp.asarray(tallies, jnp.int32))

    tallies = jnp.where(number % 4 == 0, named(heavy_load, number // 4), named(common, number - number // 4 - 1))
    mixed = jax.random.permutation(jax.random.fold_in(own, 3), count)
    source_of, sink = mixed[0:count // 2 * 2:2], mixed[1:count // 2 * 2:2]
    room = jnp.minimum(tallies[source_of] - 1, limit - tallies[sink]) // 2
    room = jnp.where((source_of == sequence[0]) | (sink == sequence[0]) | (tallies[sink] == 0), 0, jnp.maximum(room, 0))
    passed = jax.random.randint(jax.random.fold_in(own, 4), (count // 2,), 0, 1 << 20) % (room + 1)
    tallies = tallies.at[source_of].add(-passed).at[sink].add(passed)
    labels = jnp.searchsorted(jnp.cumsum(tallies), jnp.arange(rows * top), side="right").astype(jnp.int32)
    grid = labels.reshape(top, rows).T
    grid = grid[jax.random.permutation(jax.random.fold_in(own, 1), rows)]
    offset_by = jax.random.randint(jax.random.fold_in(own, 2), (rows, 1), 0, top)
    return jnp.take_along_axis(grid, (jnp.arange(top)[None, :] + offset_by) % top, axis=1)


def portions_of(count, total, bound, slope, full):
    loads = [(1 << 20) // math.isqrt(rank ** slope) + 1 for rank in range(1, count + 1)]
    largest = bound if full else min(bound, max(-(-total // count), total * loads[0] // sum(loads)))
    least = 1 if total - largest >= count - 1 else 0
    given, rest = [largest] + [least] * (count - 1), total - largest - least * (count - 1)
    while rest > 0:
        candidates = [i for i in range(1, count) if given[i] < largest] or [i for i in range(1, count) if given[i] < bound]
        whole, budget = sum([loads[i] for i in candidates]), rest
        for i in candidates:
            extra = min(bound - given[i], max(1, budget * loads[i] // whole), rest)
            given[i] = given[i] + extra
            rest = rest - extra
    return np.array(given)


def scatter_about(key, shape, spread, limit, pieces=(), kind=jnp.bfloat16):
    array = jax.random.normal(key, shape, jnp.float32) * spread
    if len(pieces) > 0:
        array = shard_levels(key, shape, pieces, -0.22, 0.18) * array
    return jnp.clip(array, min=-limit, max=limit).astype(kind)


def gaussian_with(rng, dims, scale, limit, cuts, heavy, held_as=jnp.bfloat16):
    result = scale * jax.random.normal(rng, dims, jnp.float32)
    if cuts:
        result = result * shard_levels(rng, dims, cuts, -0.22, 0.18)
    return jnp.clip(with_spikes(result, jax.random.fold_in(rng, 3), *heavy), -limit, limit).astype(held_as)


def setup_inputs(seed: int = 0) -> dict:
    splits = jax.random.split(jax.random.key(seed), 14)
    queries = draw_queries(jax.random.fold_in(splits[13], 71), 0)
    new_keys = draw_new_keys(jax.random.fold_in(splits[13], 71), 0)
    new_values = scatter_about(splits[2], (REQS, NEW, KVH * HD), 1.0, 6.0, ((0, 8),))
    cache_keys = draw_cache_keys(jax.random.fold_in(splits[13], 71), 0)
    cache_values = draw_cache_values(jax.random.fold_in(splits[13], 71), 0)
    page_table = jax.vmap(lambda own: jax.random.permutation(own, POOL_COL))(jax.random.split(splits[5], REQS)).reshape((REQS, POOL_COL)).astype(jnp.int32)
    cached_len = ragged_sizes(splits[6], REQS, REQS * MAXLEN // 4, MAXLEN, 2).astype(jnp.int32)
    moe_rows = scatter_about(splits[7], (MTOK, D), 1.0, 6.0, ((0, 8),))
    expert_ids_keys = jax.random.split(jax.random.fold_in(splits[8], 1), MTOK // TOK_EP)
    expert_ids_turns = jax.random.permutation(jax.random.fold_in(splits[8], 3), MTOK // TOK_EP)
    expert_ids = jax.vmap(lambda own, number: routed_block(jax.random.fold_in(splits[8], 2), own, number, TOK_EP, EXPERTS, TOP, CAP, 2))(expert_ids_keys, expert_ids_turns).reshape((MTOK, TOP))
    gate_probs = jnp.clip(0.1 + 0.79999997 * jax.random.uniform(splits[9], (MTOK, TOP), jnp.float32) ** shard_levels(splits[9], (MTOK, TOP), ((0, 8),), -0.2, 0.2), 0.1, 0.9)
    w_gate = scatter_about(splits[10], (N_EP, D, FF_COL), D ** -0.5, 0.09375, ((0, 8), (2, 4)))
    w_up = scatter_about(splits[11], (N_EP, D, FF_COL), D ** -0.5, 0.09375, ((0, 8), (2, 4)))
    w_down = gaussian_with(splits[12], (N_EP, FF_COL, D), FF ** -0.5, 0.09375, ((0, 8), (1, 4)), (1, 2, 4, 2.0))
    return {"queries": queries, "new_keys": new_keys, "new_values": new_values, "cache_keys": cache_keys, "cache_values": cache_values, "page_table": page_table, "cached_len": cached_len, "moe_rows": moe_rows, "expert_ids": expert_ids, "gate_probs": gate_probs, "w_gate": w_gate, "w_up": w_up, "w_down": w_down}


ROPE_BASE = 10000.0
MASKED = -1e+30

def rotary(values, positions):
    half_width = values.shape[-1] // 2
    indices = jnp.arange(half_width, dtype=jnp.float32)
    frequency = jnp.power(ROPE_BASE, -2.0 * indices / values.shape[-1])
    angles = positions.astype(jnp.float32)[:, None] * frequency[None, :]
    cosine = jnp.cos(angles)[:, None, :]
    sine_part = jnp.sin(angles)[:, None, :]
    lower_half = values[..., :half_width]
    upper_half = values[..., half_width:]
    return jnp.concatenate([lower_half * cosine - upper_half * sine_part, upper_half * cosine + lower_half * sine_part], axis=-1)

def attend_request(queries, new_keys, new_values, cache_keys, cache_values, page_row, length):
    group_size = HQ // KVH
    positions = length + jnp.arange(NEW, dtype=jnp.int32)
    q_rot = rotary(queries.astype(jnp.float32).reshape(NEW, HQ, HD), positions).astype(jnp.bfloat16)
    k_rot = rotary(new_keys.astype(jnp.float32).reshape(NEW, KVH, HD), positions).astype(jnp.bfloat16)
    cached_k = cache_keys[page_row].reshape(POOL_COL * PAGE, KVH, HD)
    cached_v = cache_values[page_row].reshape(POOL_COL * PAGE, KVH, HD)
    all_keys = jnp.concatenate([cached_k, k_rot], axis=0).astype(jnp.float32)
    all_values = jnp.concatenate([cached_v, new_values.reshape(NEW, KVH, HD)], axis=0).astype(jnp.float32)
    cache_live = jnp.arange(POOL_COL * PAGE, dtype=jnp.int32) < length
    causal = jnp.arange(NEW, dtype=jnp.int32)[None, :] <= jnp.arange(NEW, dtype=jnp.int32)[:, None]
    usable = jnp.concatenate([jnp.broadcast_to(cache_live[None, :], (NEW, POOL_COL * PAGE)), causal], axis=1)
    usable = usable[:, None, None, :]
    grouped = q_rot.astype(jnp.float32).reshape(NEW, KVH, group_size, HD)
    scores = jnp.einsum('nkgd,mkd->nkgm', grouped, all_keys) * (1.0 / math.sqrt(HD))
    scores = jnp.where(usable, scores, MASKED)
    highest = lax.optimization_barrier(jnp.max(scores, axis=-1, keepdims=True))
    weights = jnp.where(usable, jnp.exp(scores - highest), 0.0)
    row_total = lax.optimization_barrier(jnp.sum(weights, axis=-1))
    rounded = lax.optimization_barrier(weights.astype(jnp.bfloat16)).astype(jnp.float32)
    blended = jnp.einsum('nkgm,mkd->nkgd', rounded, all_values) / row_total[..., None]
    return blended.reshape(NEW, HQ * HD).astype(jnp.bfloat16)

def expert_layer(moe_rows, expert_ids, gate_probs, w_gate, w_up, w_down):
    slots_all = N_EP * CAP
    flat_ids = expert_ids.reshape(-1)
    flat_probs = jnp.concatenate([gate_probs.reshape(-1), jnp.zeros((1,), gate_probs.dtype)])
    rows_padded = jnp.concatenate([moe_rows, jnp.zeros((1, D), moe_rows.dtype)], axis=0)

    def one_expert(expert):
        entries = jnp.nonzero(flat_ids == expert, size=slots_all, fill_value=MTOK * TOP)[0].astype(jnp.int32)
        tokens = (entries // TOP).astype(jnp.int32)
        picked = rows_padded[tokens]
        gate_full = jnp.transpose(lax.dynamic_slice_in_dim(w_gate, expert * GROUP, GROUP, 0), (1, 0, 2)).reshape(D, FF)
        up_full = jnp.transpose(lax.dynamic_slice_in_dim(w_up, expert * GROUP, GROUP, 0), (1, 0, 2)).reshape(D, FF)
        down_full = lax.dynamic_slice_in_dim(w_down, expert * GROUP, GROUP, 0).reshape(FF, D)
        gate_hid = jnp.dot(picked, gate_full, preferred_element_type=jnp.float32)
        up_hid = jnp.dot(picked, up_full, preferred_element_type=jnp.float32)
        hidden = (jax.nn.silu(gate_hid) * up_hid).astype(jnp.bfloat16)
        expert_val = jnp.dot(hidden, down_full, preferred_element_type=jnp.float32)
        return (expert_val * flat_probs[entries][:, None], tokens)
    outputs, tokens = lax.map(one_expert, jnp.arange(EXPERTS, dtype=jnp.int32))
    summed = jnp.zeros((MTOK + 1, D), jnp.float32).at[tokens.reshape(-1)].add(outputs.reshape(-1, D))
    return summed[:MTOK].astype(jnp.bfloat16)

def reference(queries, new_keys, new_values, cache_keys, cache_values, page_table, cached_len, moe_rows, expert_ids, gate_probs, w_gate, w_up, w_down):
    attn_out = lax.map(lambda bundle: attend_request(*bundle), (queries, new_keys, new_values, cache_keys, cache_values, page_table, cached_len))
    moe_out = expert_layer(moe_rows, expert_ids, gate_probs, w_gate, w_up, w_down)
    return (attn_out, moe_out)
```

```python
import functools
import math

import jax
import jax.numpy as jnp
from jax import lax
from jax.experimental import pallas as pl
from jax.experimental.pallas import tpu as pltpu
from jax.sharding import PartitionSpec as P

HD = 128
EXPERTS = 8
HQ = 16
KVH = 4
PAGE = 128
CAP = 16
GROUP = HQ // KVH
K_CHUNKS = 4

ROPE_BASE = 10000.0
MASKED = -1e30
SCALE = 1.0 / math.sqrt(HD)
BF16 = jnp.bfloat16
F32 = jnp.float32
MESH = pl.DeviceIdType.MESH


def dot(a, b, dims=((1,), (0,))):
    return lax.dot_general(a, b, (dims, ((), ())), preferred_element_type=F32)


def kernel(
    n_kv,
    n_ep,
    length_ref,
    page_ref,
    queries_ref,
    new_keys_ref,
    new_values_ref,
    keys_ref,
    values_ref,
    trig_ref,
    rows_ref,
    route_ref,
    gate_hbm,
    up_hbm,
    down_hbm,
    attn_ref,
    moe_ref,
    gate_w,
    up_w,
    down_w,
    packed,
    arrived,
    gate_acc,
    up_acc,
    hidden,
    back_out,
    back_in,
    part_out,
    part_in,
    own_part,
    weights,
    blend_out,
    blend_in,
    stat_out,
    stat_in,
    final,
    gate_sem,
    up_sem,
    down_sem,
    row_send,
    row_recv,
    back_send,
    back_recv,
    part_send,
    part_recv,
    blend_send,
    blend_recv,
    stat_send,
    stat_recv,
    final_send,
    final_recv,
):
    kv = lax.axis_index("kv")
    ep = lax.axis_index("ep")
    new = queries_ref.shape[0]
    tok_rows, width = rows_ref.shape
    slots = n_ep * CAP
    depth = width // K_CHUNKS
    units = gate_acc.shape[1]
    out_width = moe_ref.shape[1]
    lanes = HQ * new // n_kv
    share = n_ep // EXPERTS

    def kv_peer(offset):
        return lax.rem(kv + offset, n_kv)

    def ep_peer(offset):
        return lax.rem(ep + offset, n_ep)

    def aligned(index, size):
        return pl.ds(pl.multiple_of(index * size, size), size)

    gate_copies = []
    up_copies = []
    for c in range(K_CHUNKS):
        part = pl.ds(c * depth, depth)
        gate_copies.append(
            pltpu.make_async_copy(gate_hbm.at[part], gate_w.at[part], gate_sem.at[c])
        )
        up_copies.append(pltpu.make_async_copy(up_hbm.at[part], up_w.at[part], up_sem.at[c]))
        gate_copies[c].start()
        up_copies[c].start()
    down_copies = []
    for i in range(n_kv):
        source = down_hbm.at[:, aligned(kv_peer(i + 1), out_width)]
        down_copies.append(pltpu.make_async_copy(source, down_w.at[i], down_sem.at[i]))
        down_copies[i].start()

    barrier = pltpu.get_barrier_semaphore()

    def greet(offset, carry):
        pl.semaphore_signal(
            barrier, inc=1, device_id={"ep": ep_peer(offset)}, device_id_type=MESH
        )
        return carry

    lax.fori_loop(1, n_ep, greet, 0)
    for offset in range(1, n_kv):
        pl.semaphore_signal(
            barrier, inc=1, device_id={"kv": kv_peer(offset)}, device_id_type=MESH
        )

    slot = lax.broadcasted_iota(jnp.int32, (slots, tok_rows), 0)
    expert = lax.div(slot, CAP * share).astype(F32)
    rank_wanted = lax.rem(slot, CAP).astype(F32)
    first = route_ref[0:1, :] == expert
    second = route_ref[1:2, :] == expert
    named = jnp.where(first | second, 1.0, 0.0)
    earlier = jnp.where(
        lax.broadcasted_iota(jnp.int32, (tok_rows, tok_rows), 0)
        < lax.broadcasted_iota(jnp.int32, (tok_rows, tok_rows), 1),
        1.0,
        0.0,
    )
    rank = dot(named.astype(BF16), earlier.astype(BF16))
    select = jnp.where(rank == rank_wanted, named, 0.0)
    prob = jnp.where(first, route_ref[2:3, :], 0.0) + jnp.where(second, route_ref[3:4, :], 0.0)
    weight = select * prob
    weight_high = weight.astype(BF16)
    weights[:, :tok_rows] = weight_high
    weights[:, tok_rows:] = (weight - weight_high.astype(F32)).astype(BF16)
    select = select.astype(BF16)
    for c in range(K_CHUNKS):
        packed[c] = dot(select, rows_ref[:, c * depth : (c + 1) * depth]).astype(BF16)
        arrived[c, aligned(ep, CAP)] = packed[c, aligned(ep, CAP)]

    pl.semaphore_wait(barrier, n_ep + n_kv - 2)

    def row_copy(c, offset):
        peer = ep_peer(offset)
        return pltpu.make_async_remote_copy(
            src_ref=packed.at[c, aligned(peer, CAP)],
            dst_ref=arrived.at[c, aligned(ep, CAP)],
            send_sem=row_send.at[c, offset],
            recv_sem=row_recv.at[c, offset],
            device_id={"ep": peer},
            device_id_type=MESH,
        )

    def row_landing(c, offset):
        source = ep_peer(n_ep - offset)
        return pltpu.make_async_remote_copy(
            src_ref=packed.at[c, aligned(source, CAP)],
            dst_ref=arrived.at[c, aligned(source, CAP)],
            send_sem=row_send.at[c, offset],
            recv_sem=row_recv.at[c, offset],
            device_id={"ep": source},
            device_id_type=MESH,
        )

    def each_peer(act):
        def step(offset, carry):
            act(offset)
            return carry

        lax.fori_loop(1, n_ep, step, 0)

    for c in range(K_CHUNKS):
        each_peer(lambda offset, c=c: row_copy(c, offset).start())

    length = length_ref[0]
    cosine = trig_ref[:, :HD]
    sine = trig_ref[:, HD:]

    def rotated(values):
        values = values.astype(F32)
        return (values * cosine + pltpu.roll(values, HD // 2, 1) * sine).astype(BF16)

    pool = keys_ref.shape[0] // PAGE
    group_lanes = GROUP * new
    live = []
    token = lax.broadcasted_iota(jnp.int32, (PAGE, group_lanes), 0)
    for s in range(pool):
        slot_id = kv * pool + s
        page = jnp.int32(0)
        for i in range(page_ref.shape[1]):
            page = page + jnp.where(page_ref[0, i] == slot_id, i, 0)
        live.append(token < length - page * PAGE)
    block = new // n_kv
    new_key = lax.broadcasted_iota(jnp.int32, (new, group_lanes), 0)
    new_query = lax.rem(lax.broadcasted_iota(jnp.int32, (new, group_lanes), 1), new)
    new_live = (new_key <= new_query) & (new_key >= kv * block) & (new_key < (kv + 1) * block)

    for g in range(KVH):
        column = slice(g * HD, (g + 1) * HD)
        grouped = jnp.concatenate(
            [
                rotated(queries_ref[:, h * HD : (h + 1) * HD])
                for h in range(g * GROUP, (g + 1) * GROUP)
            ],
            axis=0,
        )
        nt = ((1,), (1,))
        tn = ((0,), (0,))
        cached = [
            jnp.where(
                live[s],
                dot(keys_ref[s * PAGE : (s + 1) * PAGE, column], grouped, nt) * SCALE,
                MASKED,
            )
            for s in range(pool)
        ]
        fresh = jnp.where(
            new_live, dot(rotated(new_keys_ref[:, column]), grouped, nt) * SCALE, MASKED
        )
        high = jnp.max(fresh, axis=0, keepdims=True)
        for s in range(pool):
            high = jnp.maximum(high, jnp.max(cached[s], axis=0, keepdims=True))
        probs = jnp.where(new_live, jnp.exp(fresh - high), 0.0)
        total = jnp.sum(probs, axis=0, keepdims=True)
        blend = dot(new_values_ref[:, column], probs.astype(BF16), tn)
        for s in range(pool):
            probs = jnp.where(live[s], jnp.exp(cached[s] - high), 0.0)
            total = total + jnp.sum(probs, axis=0, keepdims=True)
            blend = blend + dot(
                values_ref[s * PAGE : (s + 1) * PAGE, column], probs.astype(BF16), tn
            )
        for piece in range(group_lanes // lanes):
            owner = (g * group_lanes) // lanes + piece
            cut = slice(piece * lanes, (piece + 1) * lanes)
            blend_out[owner] = blend[:, cut].astype(BF16)
            stat_out[owner, 0:1] = high[:, cut]
            stat_out[owner, 1:2] = total[:, cut]

    def blend_copies(offset):
        peer = kv_peer(offset)
        blends = pltpu.make_async_remote_copy(
            src_ref=blend_out.at[peer],
            dst_ref=blend_in.at[offset],
            send_sem=blend_send.at[offset],
            recv_sem=blend_recv.at[offset],
            device_id={"kv": peer},
            device_id_type=MESH,
        )
        stats = pltpu.make_async_remote_copy(
            src_ref=stat_out.at[peer],
            dst_ref=stat_in.at[offset],
            send_sem=stat_send.at[offset],
            recv_sem=stat_recv.at[offset],
            device_id={"kv": peer},
            device_id_type=MESH,
        )
        return blends, stats

    for offset in range(1, n_kv):
        for copy in blend_copies(offset):
            copy.start()

    chunk = min(512, units)

    def project(c):
        gate_copies[c].wait()
        up_copies[c].wait()
        each_peer(lambda offset: row_landing(c, offset).wait_recv())

        def step(n, carry):
            cols = aligned(n, chunk)
            rows = slice(c * depth, (c + 1) * depth)
            gate = dot(arrived[c], gate_w[rows, cols])
            up = dot(arrived[c], up_w[rows, cols])
            if c:
                gate = gate + gate_acc[:, cols]
                up = up + up_acc[:, cols]
            if c == K_CHUNKS - 1:
                hidden[:, cols] = (gate / (1.0 + jnp.exp(-gate)) * up).astype(BF16)
            else:
                gate_acc[:, cols] = gate
                up_acc[:, cols] = up
            return carry

        lax.fori_loop(0, units // chunk, step, 0)

    def final_copy(offset):
        peer = kv_peer(offset)
        return pltpu.make_async_remote_copy(
            src_ref=final.at[kv],
            dst_ref=final.at[kv],
            send_sem=final_send.at[offset],
            recv_sem=final_recv.at[offset],
            device_id={"kv": peer},
            device_id_type=MESH,
        )

    def final_landing(offset):
        source = kv_peer(n_kv - offset)
        return pltpu.make_async_remote_copy(
            src_ref=final.at[source],
            dst_ref=final.at[source],
            send_sem=final_send.at[offset],
            recv_sem=final_recv.at[offset],
            device_id={"kv": source},
            device_id_type=MESH,
        )

    def merge():
        for offset in range(1, n_kv):
            for copy in blend_copies(offset):
                copy.wait_recv()
        highs = [stat_out[kv, 0:1]] + [stat_in[o, 0:1] for o in range(1, n_kv)]
        totals = [stat_out[kv, 1:2]] + [stat_in[o, 1:2] for o in range(1, n_kv)]
        blends = [blend_out[kv]] + [blend_in[o] for o in range(1, n_kv)]
        highest = functools.reduce(jnp.maximum, highs)
        factors = [jnp.exp(high - highest) for high in highs]
        total = sum(f * t for f, t in zip(factors, totals))
        blended = sum(f * b.astype(F32) for f, b in zip(factors, blends))
        turned = (blended / total).T.astype(BF16)
        for h in range(lanes // new):
            final[kv, :, h * HD : (h + 1) * HD] = turned[h * new : (h + 1) * new]
        for offset in range(1, n_kv):
            final_copy(offset).start()

    project(0)
    merge()
    for c in range(1, K_CHUNKS):
        project(c)

    def back_copy(i, offset):
        peer = ep_peer(offset)
        return pltpu.make_async_remote_copy(
            src_ref=back_out.at[i, aligned(peer, CAP)],
            dst_ref=back_in.at[i, aligned(ep, CAP)],
            send_sem=back_send.at[i, offset],
            recv_sem=back_recv.at[i, offset],
            device_id={"ep": peer},
            device_id_type=MESH,
        )

    def back_landing(i, offset):
        source = ep_peer(n_ep - offset)
        return pltpu.make_async_remote_copy(
            src_ref=back_out.at[i, aligned(source, CAP)],
            dst_ref=back_in.at[i, aligned(source, CAP)],
            send_sem=back_send.at[i, offset],
            recv_sem=back_recv.at[i, offset],
            device_id={"ep": source},
            device_id_type=MESH,
        )

    out_chunk = min(512, out_width)
    for i in range(n_kv):
        down_copies[i].wait()

        def step(n, carry, i=i):
            cols = aligned(n, out_chunk)
            back_out[i, :, cols] = dot(hidden[...], down_w[i, :, cols]).astype(BF16)
            return carry

        lax.fori_loop(0, out_width // out_chunk, step, 0)
        back_in[i, aligned(ep, CAP)] = back_out[i, aligned(ep, CAP)]
        each_peer(lambda offset, i=i: back_copy(i, offset).start())

    def part_copy(i):
        return pltpu.make_async_remote_copy(
            src_ref=part_out.at[i],
            dst_ref=part_in.at[i],
            send_sem=part_send.at[i],
            recv_sem=part_recv.at[i],
            device_id={"kv": kv_peer(i + 1)},
            device_id_type=MESH,
        )

    for i in range(n_kv):
        each_peer(lambda offset, i=i: back_landing(i, offset).wait_recv())
        mixed = dot(weights[...], back_in[i], ((0,), (0,)))
        mixed = mixed[:tok_rows] + mixed[tok_rows:]
        if i < n_kv - 1:
            part_out[i] = mixed.astype(BF16)
            part_copy(i).start()
        else:
            own_part[...] = mixed

    for offset in range(1, n_kv):
        final_landing(offset).wait_recv()
    for k in range(n_kv):
        attn_ref[:, k * lanes * HD // new : (k + 1) * lanes * HD // new] = final[k]

    result = own_part[...]
    for i in range(n_kv - 1):
        part_copy(i).wait_recv()
        result = result + part_in[i].astype(F32)
    moe_ref[...] = result.astype(BF16)

    for c in range(K_CHUNKS):
        each_peer(lambda offset, c=c: row_copy(c, offset).wait_send())
    for i in range(n_kv):
        each_peer(lambda offset, i=i: back_copy(i, offset).wait_send())
    for i in range(n_kv - 1):
        part_copy(i).wait_send()
    for offset in range(1, n_kv):
        for copy in blend_copies(offset):
            copy.wait_send()
        final_copy(offset).wait_send()


def on_device(
    queries,
    new_keys,
    new_values,
    cache_keys,
    cache_values,
    page_table,
    cached_len,
    moe_rows,
    expert_ids,
    gate_probs,
    w_gate,
    w_up,
    w_down,
):
    n_kv = lax.axis_size("kv")
    n_ep = lax.axis_size("ep")
    new = queries.shape[1]
    tok_rows, width = moe_rows.shape
    units = w_gate.shape[2]
    out_width = width // n_kv
    slots = n_ep * CAP
    depth = width // K_CHUNKS
    lanes = HQ * new // n_kv

    half = HD // 2
    frequency = jnp.power(ROPE_BASE, -2.0 * jnp.arange(half, dtype=F32) / HD)
    positions = cached_len[0] + jnp.arange(new, dtype=jnp.int32)
    angles = positions.astype(F32)[:, None] * frequency[None, :]
    cosine = jnp.cos(angles)
    sine = jnp.sin(angles)
    trig = jnp.concatenate([cosine, cosine, -sine, sine], axis=1)
    route = jnp.concatenate([expert_ids.T.astype(F32), gate_probs.T], axis=0)

    vmem = pl.BlockSpec(memory_space=pltpu.VMEM)
    smem = pl.BlockSpec(memory_space=pltpu.SMEM)
    hbm = pl.BlockSpec(memory_space=pl.ANY)
    dma = pltpu.SemaphoreType.DMA
    attn_out, moe_out = pl.pallas_call(
        functools.partial(kernel, n_kv, n_ep),
        out_shape=(
            jax.ShapeDtypeStruct((new, HQ * HD), BF16),
            jax.ShapeDtypeStruct((tok_rows, out_width), BF16),
        ),
        in_specs=[smem, smem] + [vmem] * 8 + [hbm] * 3,
        out_specs=(vmem, vmem),
        scratch_shapes=[
            pltpu.VMEM((width, units), BF16),
            pltpu.VMEM((width, units), BF16),
            pltpu.VMEM((n_kv, units, out_width), BF16),
            pltpu.VMEM((K_CHUNKS, slots, depth), BF16),
            pltpu.VMEM((K_CHUNKS, slots, depth), BF16),
            pltpu.VMEM((slots, units), F32),
            pltpu.VMEM((slots, units), F32),
            pltpu.VMEM((slots, units), BF16),
            pltpu.VMEM((n_kv, slots, out_width), BF16),
            pltpu.VMEM((n_kv, slots, out_width), BF16),
            pltpu.VMEM((n_kv - 1, tok_rows, out_width), BF16),
            pltpu.VMEM((n_kv - 1, tok_rows, out_width), BF16),
            pltpu.VMEM((tok_rows, out_width), F32),
            pltpu.VMEM((slots, 2 * tok_rows), BF16),
            pltpu.VMEM((n_kv, HD, lanes), BF16),
            pltpu.VMEM((n_kv, HD, lanes), BF16),
            pltpu.VMEM((n_kv, 8, lanes), F32),
            pltpu.VMEM((n_kv, 8, lanes), F32),
            pltpu.VMEM((n_kv, new, HQ * HD // n_kv), BF16),
            dma((K_CHUNKS,)),
            dma((K_CHUNKS,)),
            dma((n_kv,)),
            dma((K_CHUNKS, n_ep)),
            dma((K_CHUNKS, n_ep)),
            dma((n_kv, n_ep)),
            dma((n_kv, n_ep)),
            dma((n_kv,)),
            dma((n_kv,)),
            dma((n_kv,)),
            dma((n_kv,)),
            dma((n_kv,)),
            dma((n_kv,)),
            dma((n_kv,)),
            dma((n_kv,)),
        ],
        compiler_params=pltpu.CompilerParams(
            collective_id=0, has_side_effects=True, vmem_limit_bytes=60 * 1024 * 1024
        ),
    )(
        cached_len,
        page_table,
        queries[0],
        new_keys[0],
        new_values[0],
        cache_keys.reshape(-1, KVH * HD),
        cache_values.reshape(-1, KVH * HD),
        trig,
        moe_rows,
        route,
        w_gate[0],
        w_up[0],
        w_down[0],
    )
    return attn_out[None], moe_out


def solution(mesh):
    return jax.shard_map(
        on_device,
        mesh=mesh,
        in_specs=(
            P("ep", None, None),
            P("ep", None, None),
            P("ep", None, None),
            P("ep", "kv", None, None),
            P("ep", "kv", None, None),
            P("ep", None),
            P("ep"),
            P("ep", None),
            P("ep", None),
            P("ep", None),
            P("ep", None, "kv"),
            P("ep", None, "kv"),
            P("ep", "kv", None),
        ),
        out_specs=(P("ep", None, None), P("ep", "kv")),
        check_vma=False,
    )
```

```python
import functools
import math

import jax
import jax.numpy as jnp
from jax import lax
from jax.experimental import pallas as pl
from jax.experimental.pallas import tpu as pltpu
from jax.sharding import PartitionSpec as P

HD = 128
EXPERTS = 8
HQ = 16
KVH = 4
PAGE = 128
CAP = 16
GROUP = HQ // KVH
K_CHUNKS = 4

ROPE_BASE = 10000.0
MASKED = -1e30
SCALE = 1.0 / math.sqrt(HD)
BF16 = jnp.bfloat16
F32 = jnp.float32
MESH = pl.DeviceIdType.MESH


def dot(a, b, dims=((1,), (0,))):
    return lax.dot_general(a, b, (dims, ((), ())), preferred_element_type=F32)


def kernel(
    n_kv,
    n_ep,
    length_ref,
    page_ref,
    queries_ref,
    new_keys_ref,
    new_values_ref,
    keys_ref,
    values_ref,
    cos_ref,
    sin_ref,
    rows_ref,
    ids_ref,
    probs_ref,
    gate_hbm,
    up_hbm,
    down_hbm,
    attn_ref,
    moe_ref,
    gate_w,
    up_w,
    down_w,
    packed,
    arrived,
    gate_acc,
    up_acc,
    hidden,
    back_out,
    back_in,
    part_out,
    part_in,
    own_part,
    weights,
    blend_out,
    blend_in,
    stat_out,
    stat_in,
    final,
    gate_sem,
    up_sem,
    down_sem,
    row_send,
    row_recv,
    back_send,
    back_recv,
    part_send,
    part_recv,
    blend_send,
    blend_recv,
    stat_send,
    stat_recv,
    final_send,
    final_recv,
):
    kv = lax.axis_index("kv")
    ep = lax.axis_index("ep")
    new = queries_ref.shape[0]
    tok_rows, width = rows_ref.shape
    slots = n_ep * CAP
    depth = width // K_CHUNKS
    units = gate_acc.shape[1]
    out_width = moe_ref.shape[1]
    lanes = HQ * new // n_kv
    share = n_ep // EXPERTS

    def kv_peer(offset):
        return lax.rem(kv + offset, n_kv)

    def ep_peer(offset):
        return lax.rem(ep + offset, n_ep)

    def aligned(index, size):
        return pl.ds(pl.multiple_of(index * size, size), size)

    gate_copies = []
    up_copies = []
    for c in range(K_CHUNKS):
        part = pl.ds(c * depth, depth)
        gate_copies.append(
            pltpu.make_async_copy(gate_hbm.at[part], gate_w.at[part], gate_sem.at[c])
        )
        up_copies.append(pltpu.make_async_copy(up_hbm.at[part], up_w.at[part], up_sem.at[c]))
        gate_copies[c].start()
        up_copies[c].start()
    down_copies = []
    for i in range(n_kv):
        source = down_hbm.at[:, aligned(kv_peer(i + 1), out_width)]
        down_copies.append(pltpu.make_async_copy(source, down_w.at[i], down_sem.at[i]))
        down_copies[i].start()

    barrier = pltpu.get_barrier_semaphore()

    def greet(offset, carry):
        pl.semaphore_signal(
            barrier, inc=1, device_id={"ep": ep_peer(offset)}, device_id_type=MESH
        )
        return carry

    lax.fori_loop(1, n_ep, greet, 0)
    for offset in range(1, n_kv):
        pl.semaphore_signal(
            barrier, inc=1, device_id={"kv": kv_peer(offset)}, device_id_type=MESH
        )

    slot = lax.broadcasted_iota(jnp.int32, (slots, tok_rows), 0)
    expert = lax.div(slot, CAP * share)
    rank_wanted = lax.rem(slot, CAP).astype(F32)
    first = ids_ref[0:1, :] == expert
    second = ids_ref[1:2, :] == expert
    named = jnp.where(first | second, 1.0, 0.0)
    earlier = jnp.where(
        lax.broadcasted_iota(jnp.int32, (tok_rows, tok_rows), 0)
        < lax.broadcasted_iota(jnp.int32, (tok_rows, tok_rows), 1),
        1.0,
        0.0,
    )
    rank = dot(named.astype(BF16), earlier.astype(BF16))
    select = jnp.where(rank == rank_wanted, named, 0.0)
    prob = jnp.where(first, probs_ref[0:1, :], 0.0) + jnp.where(second, probs_ref[1:2, :], 0.0)
    weight = select * prob
    weight_high = weight.astype(BF16)
    weights[:, :tok_rows] = weight_high
    weights[:, tok_rows:] = (weight - weight_high.astype(F32)).astype(BF16)
    select = select.astype(BF16)
    for c in range(K_CHUNKS):
        packed[c] = dot(select, rows_ref[:, c * depth : (c + 1) * depth]).astype(BF16)
        arrived[c, aligned(ep, CAP)] = packed[c, aligned(ep, CAP)]

    pl.semaphore_wait(barrier, n_ep + n_kv - 2)

    def row_copy(c, offset):
        peer = ep_peer(offset)
        return pltpu.make_async_remote_copy(
            src_ref=packed.at[c, aligned(peer, CAP)],
            dst_ref=arrived.at[c, aligned(ep, CAP)],
            send_sem=row_send.at[c, offset],
            recv_sem=row_recv.at[c, offset],
            device_id={"ep": peer},
            device_id_type=MESH,
        )

    def row_landing(c, offset):
        source = ep_peer(n_ep - offset)
        return pltpu.make_async_remote_copy(
            src_ref=packed.at[c, aligned(source, CAP)],
            dst_ref=arrived.at[c, aligned(source, CAP)],
            send_sem=row_send.at[c, offset],
            recv_sem=row_recv.at[c, offset],
            device_id={"ep": source},
            device_id_type=MESH,
        )

    def each_peer(act):
        def step(offset, carry):
            act(offset)
            return carry

        lax.fori_loop(1, n_ep, step, 0)

    for c in range(K_CHUNKS):
        each_peer(lambda offset, c=c: row_copy(c, offset).start())

    length = length_ref[0]
    cosine = jnp.concatenate([cos_ref[...], cos_ref[...]], axis=1)
    sine = jnp.concatenate([-sin_ref[...], sin_ref[...]], axis=1)

    def rotated(values):
        values = values.astype(F32)
        return (values * cosine + pltpu.roll(values, HD // 2, 1) * sine).astype(BF16)

    pool = keys_ref.shape[0] // PAGE
    group_lanes = GROUP * new
    live = []
    token = lax.broadcasted_iota(jnp.int32, (PAGE, group_lanes), 0)
    for s in range(pool):
        slot_id = kv * pool + s
        page = jnp.int32(0)
        for i in range(page_ref.shape[1]):
            page = page + jnp.where(page_ref[0, i] == slot_id, i, 0)
        live.append(token < length - page * PAGE)
    block = new // n_kv
    new_key = lax.broadcasted_iota(jnp.int32, (new, group_lanes), 0)
    new_query = lax.rem(lax.broadcasted_iota(jnp.int32, (new, group_lanes), 1), new)
    new_live = (new_key <= new_query) & (new_key >= kv * block) & (new_key < (kv + 1) * block)

    for g in range(KVH):
        column = slice(g * HD, (g + 1) * HD)
        grouped = jnp.concatenate(
            [
                rotated(queries_ref[:, h * HD : (h + 1) * HD])
                for h in range(g * GROUP, (g + 1) * GROUP)
            ],
            axis=0,
        )
        nt = ((1,), (1,))
        tn = ((0,), (0,))
        cached = [
            jnp.where(
                live[s],
                dot(keys_ref[s * PAGE : (s + 1) * PAGE, column], grouped, nt) * SCALE,
                MASKED,
            )
            for s in range(pool)
        ]
        fresh = jnp.where(
            new_live, dot(rotated(new_keys_ref[:, column]), grouped, nt) * SCALE, MASKED
        )
        high = jnp.max(fresh, axis=0, keepdims=True)
        for s in range(pool):
            high = jnp.maximum(high, jnp.max(cached[s], axis=0, keepdims=True))
        probs = jnp.where(new_live, jnp.exp(fresh - high), 0.0)
        total = jnp.sum(probs, axis=0, keepdims=True)
        blend = dot(new_values_ref[:, column], probs.astype(BF16), tn)
        for s in range(pool):
            probs = jnp.where(live[s], jnp.exp(cached[s] - high), 0.0)
            total = total + jnp.sum(probs, axis=0, keepdims=True)
            blend = blend + dot(
                values_ref[s * PAGE : (s + 1) * PAGE, column], probs.astype(BF16), tn
            )
        for piece in range(group_lanes // lanes):
            owner = (g * group_lanes) // lanes + piece
            cut = slice(piece * lanes, (piece + 1) * lanes)
            blend_out[owner] = blend[:, cut].astype(BF16)
            stat_out[owner, 0:1] = high[:, cut]
            stat_out[owner, 1:2] = total[:, cut]

    def blend_copies(offset):
        peer = kv_peer(offset)
        blends = pltpu.make_async_remote_copy(
            src_ref=blend_out.at[peer],
            dst_ref=blend_in.at[offset],
            send_sem=blend_send.at[offset],
            recv_sem=blend_recv.at[offset],
            device_id={"kv": peer},
            device_id_type=MESH,
        )
        stats = pltpu.make_async_remote_copy(
            src_ref=stat_out.at[peer],
            dst_ref=stat_in.at[offset],
            send_sem=stat_send.at[offset],
            recv_sem=stat_recv.at[offset],
            device_id={"kv": peer},
            device_id_type=MESH,
        )
        return blends, stats

    for offset in range(1, n_kv):
        for copy in blend_copies(offset):
            copy.start()

    chunk = min(512, units)

    def project(c):
        gate_copies[c].wait()
        up_copies[c].wait()
        each_peer(lambda offset: row_landing(c, offset).wait_recv())

        def step(n, carry):
            cols = aligned(n, chunk)
            rows = slice(c * depth, (c + 1) * depth)
            gate = dot(arrived[c], gate_w[rows, cols])
            up = dot(arrived[c], up_w[rows, cols])
            if c:
                gate = gate + gate_acc[:, cols]
                up = up + up_acc[:, cols]
            if c == K_CHUNKS - 1:
                hidden[:, cols] = (gate / (1.0 + jnp.exp(-gate)) * up).astype(BF16)
            else:
                gate_acc[:, cols] = gate
                up_acc[:, cols] = up
            return carry

        lax.fori_loop(0, units // chunk, step, 0)

    def final_copy(offset):
        peer = kv_peer(offset)
        return pltpu.make_async_remote_copy(
            src_ref=final.at[kv],
            dst_ref=final.at[kv],
            send_sem=final_send.at[offset],
            recv_sem=final_recv.at[offset],
            device_id={"kv": peer},
            device_id_type=MESH,
        )

    def final_landing(offset):
        source = kv_peer(n_kv - offset)
        return pltpu.make_async_remote_copy(
            src_ref=final.at[source],
            dst_ref=final.at[source],
            send_sem=final_send.at[offset],
            recv_sem=final_recv.at[offset],
            device_id={"kv": source},
            device_id_type=MESH,
        )

    def merge():
        for offset in range(1, n_kv):
            for copy in blend_copies(offset):
                copy.wait_recv()
        highs = [stat_out[kv, 0:1]] + [stat_in[o, 0:1] for o in range(1, n_kv)]
        totals = [stat_out[kv, 1:2]] + [stat_in[o, 1:2] for o in range(1, n_kv)]
        blends = [blend_out[kv]] + [blend_in[o] for o in range(1, n_kv)]
        highest = functools.reduce(jnp.maximum, highs)
        factors = [jnp.exp(high - highest) for high in highs]
        total = sum(f * t for f, t in zip(factors, totals))
        blended = sum(f * b.astype(F32) for f, b in zip(factors, blends))
        turned = (blended / total).T.astype(BF16)
        for h in range(lanes // new):
            final[kv, :, h * HD : (h + 1) * HD] = turned[h * new : (h + 1) * new]
        for offset in range(1, n_kv):
            final_copy(offset).start()

    project(0)
    merge()
    for c in range(1, K_CHUNKS):
        project(c)

    def back_copy(i, offset):
        peer = ep_peer(offset)
        return pltpu.make_async_remote_copy(
            src_ref=back_out.at[i, aligned(peer, CAP)],
            dst_ref=back_in.at[i, aligned(ep, CAP)],
            send_sem=back_send.at[i, offset],
            recv_sem=back_recv.at[i, offset],
            device_id={"ep": peer},
            device_id_type=MESH,
        )

    def back_landing(i, offset):
        source = ep_peer(n_ep - offset)
        return pltpu.make_async_remote_copy(
            src_ref=back_out.at[i, aligned(source, CAP)],
            dst_ref=back_in.at[i, aligned(source, CAP)],
            send_sem=back_send.at[i, offset],
            recv_sem=back_recv.at[i, offset],
            device_id={"ep": source},
            device_id_type=MESH,
        )

    out_chunk = min(512, out_width)
    for i in range(n_kv):
        down_copies[i].wait()

        def step(n, carry, i=i):
            cols = aligned(n, out_chunk)
            back_out[i, :, cols] = dot(hidden[...], down_w[i, :, cols]).astype(BF16)
            return carry

        lax.fori_loop(0, out_width // out_chunk, step, 0)
        back_in[i, aligned(ep, CAP)] = back_out[i, aligned(ep, CAP)]
        each_peer(lambda offset, i=i: back_copy(i, offset).start())

    def part_copy(i):
        return pltpu.make_async_remote_copy(
            src_ref=part_out.at[i],
            dst_ref=part_in.at[i],
            send_sem=part_send.at[i],
            recv_sem=part_recv.at[i],
            device_id={"kv": kv_peer(i + 1)},
            device_id_type=MESH,
        )

    for i in range(n_kv):
        each_peer(lambda offset, i=i: back_landing(i, offset).wait_recv())
        mixed = dot(weights[...], back_in[i], ((0,), (0,)))
        mixed = mixed[:tok_rows] + mixed[tok_rows:]
        if i < n_kv - 1:
            part_out[i] = mixed.astype(BF16)
            part_copy(i).start()
        else:
            own_part[...] = mixed

    for offset in range(1, n_kv):
        final_landing(offset).wait_recv()
    for k in range(n_kv):
        attn_ref[:, k * lanes * HD // new : (k + 1) * lanes * HD // new] = final[k]

    result = own_part[...]
    for i in range(n_kv - 1):
        part_copy(i).wait_recv()
        result = result + part_in[i].astype(F32)
    moe_ref[...] = result.astype(BF16)

    for c in range(K_CHUNKS):
        each_peer(lambda offset, c=c: row_copy(c, offset).wait_send())
    for i in range(n_kv):
        each_peer(lambda offset, i=i: back_copy(i, offset).wait_send())
    for i in range(n_kv - 1):
        part_copy(i).wait_send()
    for offset in range(1, n_kv):
        for copy in blend_copies(offset):
            copy.wait_send()
        final_copy(offset).wait_send()


def on_device(
    queries,
    new_keys,
    new_values,
    cache_keys,
    cache_values,
    page_table,
    cached_len,
    moe_rows,
    expert_ids,
    gate_probs,
    w_gate,
    w_up,
    w_down,
):
    n_kv = lax.axis_size("kv")
    n_ep = lax.axis_size("ep")
    new = queries.shape[1]
    tok_rows, width = moe_rows.shape
    units = w_gate.shape[2]
    out_width = width // n_kv
    slots = n_ep * CAP
    depth = width // K_CHUNKS
    lanes = HQ * new // n_kv

    half = HD // 2
    frequency = jnp.power(ROPE_BASE, -2.0 * jnp.arange(half, dtype=F32) / HD)
    positions = cached_len[0] + jnp.arange(new, dtype=jnp.int32)
    angles = positions.astype(F32)[:, None] * frequency[None, :]
    cosine = jnp.cos(angles)
    sine = jnp.sin(angles)

    vmem = pl.BlockSpec(memory_space=pltpu.VMEM)
    smem = pl.BlockSpec(memory_space=pltpu.SMEM)
    hbm = pl.BlockSpec(memory_space=pl.ANY)
    dma = pltpu.SemaphoreType.DMA
    attn_out, moe_out = pl.pallas_call(
        functools.partial(kernel, n_kv, n_ep),
        out_shape=(
            jax.ShapeDtypeStruct((new, HQ * HD), BF16),
            jax.ShapeDtypeStruct((tok_rows, out_width), BF16),
        ),
        in_specs=[smem, smem] + [vmem] * 10 + [hbm] * 3,
        out_specs=(vmem, vmem),
        scratch_shapes=[
            pltpu.VMEM((width, units), BF16),
            pltpu.VMEM((width, units), BF16),
            pltpu.VMEM((n_kv, units, out_width), BF16),
            pltpu.VMEM((K_CHUNKS, slots, depth), BF16),
            pltpu.VMEM((K_CHUNKS, slots, depth), BF16),
            pltpu.VMEM((slots, units), F32),
            pltpu.VMEM((slots, units), F32),
            pltpu.VMEM((slots, units), BF16),
            pltpu.VMEM((n_kv, slots, out_width), BF16),
            pltpu.VMEM((n_kv, slots, out_width), BF16),
            pltpu.VMEM((n_kv - 1, tok_rows, out_width), BF16),
            pltpu.VMEM((n_kv - 1, tok_rows, out_width), BF16),
            pltpu.VMEM((tok_rows, out_width), F32),
            pltpu.VMEM((slots, 2 * tok_rows), BF16),
            pltpu.VMEM((n_kv, HD, lanes), BF16),
            pltpu.VMEM((n_kv, HD, lanes), BF16),
            pltpu.VMEM((n_kv, 8, lanes), F32),
            pltpu.VMEM((n_kv, 8, lanes), F32),
            pltpu.VMEM((n_kv, new, HQ * HD // n_kv), BF16),
            dma((K_CHUNKS,)),
            dma((K_CHUNKS,)),
            dma((n_kv,)),
            dma((K_CHUNKS, n_ep)),
            dma((K_CHUNKS, n_ep)),
            dma((n_kv, n_ep)),
            dma((n_kv, n_ep)),
            dma((n_kv,)),
            dma((n_kv,)),
            dma((n_kv,)),
            dma((n_kv,)),
            dma((n_kv,)),
            dma((n_kv,)),
            dma((n_kv,)),
            dma((n_kv,)),
        ],
        compiler_params=pltpu.CompilerParams(
            collective_id=0, has_side_effects=True, vmem_limit_bytes=60 * 1024 * 1024
        ),
    )(
        cached_len,
        page_table,
        queries[0],
        new_keys[0],
        new_values[0],
        cache_keys.reshape(-1, KVH * HD),
        cache_values.reshape(-1, KVH * HD),
        cosine,
        sine,
        moe_rows,
        expert_ids.T,
        gate_probs.T,
        w_gate[0],
        w_up[0],
        w_down[0],
    )
    return attn_out[None], moe_out


def solution(mesh):
    return jax.shard_map(
        on_device,
        mesh=mesh,
        in_specs=(
            P("ep", None, None),
            P("ep", None, None),
            P("ep", None, None),
            P("ep", "kv", None, None),
            P("ep", "kv", None, None),
            P("ep", None),
            P("ep"),
            P("ep", None),
            P("ep", None),
            P("ep", None),
            P("ep", None, "kv"),
            P("ep", None, "kv"),
            P("ep", "kv", None),
        ),
        out_specs=(P("ep", None, None), P("ep", "kv")),
        check_vma=False,
    )
```

```python
import functools
import math

import jax
import jax.numpy as jnp
from jax import lax
from jax.experimental import pallas as pl
from jax.experimental.pallas import tpu as pltpu
from jax.sharding import PartitionSpec as P

HD = 128
EXPERTS = 8
HQ = 16
KVH = 4
PAGE = 128
CAP = 16
GROUP = HQ // KVH
K_CHUNKS = 4

ROPE_BASE = 10000.0
MASKED = -1e30
SCALE = 1.0 / math.sqrt(HD)
BF16 = jnp.bfloat16
F32 = jnp.float32
MESH = pl.DeviceIdType.MESH


def dot(a, b, dims=((1,), (0,))):
    return lax.dot_general(a, b, (dims, ((), ())), preferred_element_type=F32)


def kernel(
    n_kv,
    n_ep,
    length_ref,
    page_ref,
    queries_hbm,
    new_keys_hbm,
    new_values_hbm,
    keys_hbm,
    values_hbm,
    cos_ref,
    sin_ref,
    rows_ref,
    ids_ref,
    probs_ref,
    gate_hbm,
    up_hbm,
    down_hbm,
    attn_hbm,
    moe_ref,
    queries_ref,
    new_keys_ref,
    new_values_ref,
    keys_ref,
    values_ref,
    gate_w,
    up_w,
    down_w,
    packed,
    arrived,
    gate_acc,
    up_acc,
    hidden,
    back_out,
    back_in,
    part_out,
    part_in,
    own_part,
    weights,
    blend_out,
    blend_in,
    stat_out,
    stat_in,
    final,
    load_sem,
    store_sem,
    gate_sem,
    up_sem,
    down_sem,
    row_send,
    row_recv,
    back_send,
    back_recv,
    part_send,
    part_recv,
    blend_send,
    blend_recv,
    stat_send,
    stat_recv,
    final_send,
    final_recv,
):
    kv = lax.axis_index("kv")
    ep = lax.axis_index("ep")
    new = queries_ref.shape[0]
    tok_rows, width = rows_ref.shape
    slots = n_ep * CAP
    depth = width // K_CHUNKS
    units = gate_acc.shape[1]
    out_width = moe_ref.shape[1]
    lanes = HQ * new // n_kv
    share = n_ep // EXPERTS

    def kv_peer(offset):
        return lax.rem(kv + offset, n_kv)

    def ep_peer(offset):
        return lax.rem(ep + offset, n_ep)

    def aligned(index, size):
        return pl.ds(pl.multiple_of(index * size, size), size)

    loads = [
        pltpu.make_async_copy(source, target, load_sem.at[i])
        for i, (source, target) in enumerate(
            [
                (queries_hbm, queries_ref),
                (new_keys_hbm, new_keys_ref),
                (new_values_hbm, new_values_ref),
                (keys_hbm, keys_ref),
                (values_hbm, values_ref),
            ]
        )
    ]
    for load in loads:
        load.start()

    gate_copies = []
    up_copies = []
    for c in range(K_CHUNKS):
        part = pl.ds(c * depth, depth)
        gate_copies.append(
            pltpu.make_async_copy(gate_hbm.at[part], gate_w.at[part], gate_sem.at[c])
        )
        up_copies.append(pltpu.make_async_copy(up_hbm.at[part], up_w.at[part], up_sem.at[c]))
        gate_copies[c].start()
        up_copies[c].start()
    down_copies = []
    for i in range(n_kv):
        source = down_hbm.at[:, aligned(kv_peer(i + 1), out_width)]
        down_copies.append(pltpu.make_async_copy(source, down_w.at[i], down_sem.at[i]))
        down_copies[i].start()

    barrier = pltpu.get_barrier_semaphore()

    def greet(offset, carry):
        pl.semaphore_signal(
            barrier, inc=1, device_id={"ep": ep_peer(offset)}, device_id_type=MESH
        )
        return carry

    lax.fori_loop(1, n_ep, greet, 0)
    for offset in range(1, n_kv):
        pl.semaphore_signal(
            barrier, inc=1, device_id={"kv": kv_peer(offset)}, device_id_type=MESH
        )

    slot = lax.broadcasted_iota(jnp.int32, (slots, tok_rows), 0)
    expert = lax.div(slot, CAP * share)
    rank_wanted = lax.rem(slot, CAP).astype(F32)
    first = ids_ref[0:1, :] == expert
    second = ids_ref[1:2, :] == expert
    named = jnp.where(first | second, 1.0, 0.0)
    earlier = jnp.where(
        lax.broadcasted_iota(jnp.int32, (tok_rows, tok_rows), 0)
        < lax.broadcasted_iota(jnp.int32, (tok_rows, tok_rows), 1),
        1.0,
        0.0,
    )
    rank = dot(named.astype(BF16), earlier.astype(BF16))
    select = jnp.where(rank == rank_wanted, named, 0.0)
    prob = jnp.where(first, probs_ref[0:1, :], 0.0) + jnp.where(second, probs_ref[1:2, :], 0.0)
    weight = select * prob
    weight_high = weight.astype(BF16)
    weights[:, :tok_rows] = weight_high
    weights[:, tok_rows:] = (weight - weight_high.astype(F32)).astype(BF16)
    select = select.astype(BF16)
    for c in range(K_CHUNKS):
        packed[c] = dot(select, rows_ref[:, c * depth : (c + 1) * depth]).astype(BF16)
        arrived[c, aligned(ep, CAP)] = packed[c, aligned(ep, CAP)]

    pl.semaphore_wait(barrier, n_ep + n_kv - 2)

    def row_copy(c, offset):
        peer = ep_peer(offset)
        return pltpu.make_async_remote_copy(
            src_ref=packed.at[c, aligned(peer, CAP)],
            dst_ref=arrived.at[c, aligned(ep, CAP)],
            send_sem=row_send.at[c, offset],
            recv_sem=row_recv.at[c, offset],
            device_id={"ep": peer},
            device_id_type=MESH,
        )

    def row_landing(c, offset):
        source = ep_peer(n_ep - offset)
        return pltpu.make_async_remote_copy(
            src_ref=packed.at[c, aligned(source, CAP)],
            dst_ref=arrived.at[c, aligned(source, CAP)],
            send_sem=row_send.at[c, offset],
            recv_sem=row_recv.at[c, offset],
            device_id={"ep": source},
            device_id_type=MESH,
        )

    def each_peer(act):
        def step(offset, carry):
            act(offset)
            return carry

        lax.fori_loop(1, n_ep, step, 0)

    for c in range(K_CHUNKS):
        each_peer(lambda offset, c=c: row_copy(c, offset).start())

    for load in loads:
        load.wait()
    length = length_ref[0]
    cosine = jnp.concatenate([cos_ref[...], cos_ref[...]], axis=1)
    sine = jnp.concatenate([-sin_ref[...], sin_ref[...]], axis=1)

    def rotated(values):
        values = values.astype(F32)
        return (values * cosine + pltpu.roll(values, HD // 2, 1) * sine).astype(BF16)

    pool = keys_ref.shape[0] // PAGE
    group_lanes = GROUP * new
    live = []
    token = lax.broadcasted_iota(jnp.int32, (PAGE, group_lanes), 0)
    for s in range(pool):
        slot_id = kv * pool + s
        page = jnp.int32(0)
        for i in range(page_ref.shape[1]):
            page = page + jnp.where(page_ref[0, i] == slot_id, i, 0)
        live.append(token < length - page * PAGE)
    block = new // n_kv
    new_key = lax.broadcasted_iota(jnp.int32, (new, group_lanes), 0)
    new_query = lax.rem(lax.broadcasted_iota(jnp.int32, (new, group_lanes), 1), new)
    new_live = (new_key <= new_query) & (new_key >= kv * block) & (new_key < (kv + 1) * block)

    for g in range(KVH):
        column = slice(g * HD, (g + 1) * HD)
        grouped = jnp.concatenate(
            [
                rotated(queries_ref[:, h * HD : (h + 1) * HD])
                for h in range(g * GROUP, (g + 1) * GROUP)
            ],
            axis=0,
        )
        nt = ((1,), (1,))
        tn = ((0,), (0,))
        cached = [
            jnp.where(
                live[s],
                dot(keys_ref[s * PAGE : (s + 1) * PAGE, column], grouped, nt) * SCALE,
                MASKED,
            )
            for s in range(pool)
        ]
        fresh = jnp.where(
            new_live, dot(rotated(new_keys_ref[:, column]), grouped, nt) * SCALE, MASKED
        )
        high = jnp.max(fresh, axis=0, keepdims=True)
        for s in range(pool):
            high = jnp.maximum(high, jnp.max(cached[s], axis=0, keepdims=True))
        probs = jnp.where(new_live, jnp.exp(fresh - high), 0.0)
        total = jnp.sum(probs, axis=0, keepdims=True)
        blend = dot(new_values_ref[:, column], probs.astype(BF16), tn)
        for s in range(pool):
            probs = jnp.where(live[s], jnp.exp(cached[s] - high), 0.0)
            total = total + jnp.sum(probs, axis=0, keepdims=True)
            blend = blend + dot(
                values_ref[s * PAGE : (s + 1) * PAGE, column], probs.astype(BF16), tn
            )
        for piece in range(group_lanes // lanes):
            owner = (g * group_lanes) // lanes + piece
            cut = slice(piece * lanes, (piece + 1) * lanes)
            blend_out[owner] = blend[:, cut].astype(BF16)
            stat_out[owner, 0:1] = high[:, cut]
            stat_out[owner, 1:2] = total[:, cut]

    def blend_copies(offset):
        peer = kv_peer(offset)
        blends = pltpu.make_async_remote_copy(
            src_ref=blend_out.at[peer],
            dst_ref=blend_in.at[offset],
            send_sem=blend_send.at[offset],
            recv_sem=blend_recv.at[offset],
            device_id={"kv": peer},
            device_id_type=MESH,
        )
        stats = pltpu.make_async_remote_copy(
            src_ref=stat_out.at[peer],
            dst_ref=stat_in.at[offset],
            send_sem=stat_send.at[offset],
            recv_sem=stat_recv.at[offset],
            device_id={"kv": peer},
            device_id_type=MESH,
        )
        return blends, stats

    for offset in range(1, n_kv):
        for copy in blend_copies(offset):
            copy.start()

    chunk = min(512, units)

    def project(c):
        gate_copies[c].wait()
        up_copies[c].wait()
        each_peer(lambda offset: row_landing(c, offset).wait_recv())

        def step(n, carry):
            cols = aligned(n, chunk)
            rows = slice(c * depth, (c + 1) * depth)
            gate = dot(arrived[c], gate_w[rows, cols])
            up = dot(arrived[c], up_w[rows, cols])
            if c:
                gate = gate + gate_acc[:, cols]
                up = up + up_acc[:, cols]
            if c == K_CHUNKS - 1:
                hidden[:, cols] = (gate / (1.0 + jnp.exp(-gate)) * up).astype(BF16)
            else:
                gate_acc[:, cols] = gate
                up_acc[:, cols] = up
            return carry

        lax.fori_loop(0, units // chunk, step, 0)

    def final_copy(offset):
        peer = kv_peer(offset)
        return pltpu.make_async_remote_copy(
            src_ref=final.at[kv],
            dst_ref=final.at[kv],
            send_sem=final_send.at[offset],
            recv_sem=final_recv.at[offset],
            device_id={"kv": peer},
            device_id_type=MESH,
        )

    def final_landing(offset):
        source = kv_peer(n_kv - offset)
        return pltpu.make_async_remote_copy(
            src_ref=final.at[source],
            dst_ref=final.at[source],
            send_sem=final_send.at[offset],
            recv_sem=final_recv.at[offset],
            device_id={"kv": source},
            device_id_type=MESH,
        )

    def merge():
        for offset in range(1, n_kv):
            for copy in blend_copies(offset):
                copy.wait_recv()
        highs = [stat_out[kv, 0:1]] + [stat_in[o, 0:1] for o in range(1, n_kv)]
        totals = [stat_out[kv, 1:2]] + [stat_in[o, 1:2] for o in range(1, n_kv)]
        blends = [blend_out[kv]] + [blend_in[o] for o in range(1, n_kv)]
        highest = functools.reduce(jnp.maximum, highs)
        factors = [jnp.exp(high - highest) for high in highs]
        total = sum(f * t for f, t in zip(factors, totals))
        blended = sum(f * b.astype(F32) for f, b in zip(factors, blends))
        turned = (blended / total).T.astype(BF16)
        for h in range(lanes // new):
            final[kv, :, h * HD : (h + 1) * HD] = turned[h * new : (h + 1) * new]
        for offset in range(1, n_kv):
            final_copy(offset).start()

    project(0)
    merge()
    for c in range(1, K_CHUNKS):
        project(c)

    def back_copy(i, offset):
        peer = ep_peer(offset)
        return pltpu.make_async_remote_copy(
            src_ref=back_out.at[i, aligned(peer, CAP)],
            dst_ref=back_in.at[i, aligned(ep, CAP)],
            send_sem=back_send.at[i, offset],
            recv_sem=back_recv.at[i, offset],
            device_id={"ep": peer},
            device_id_type=MESH,
        )

    def back_landing(i, offset):
        source = ep_peer(n_ep - offset)
        return pltpu.make_async_remote_copy(
            src_ref=back_out.at[i, aligned(source, CAP)],
            dst_ref=back_in.at[i, aligned(source, CAP)],
            send_sem=back_send.at[i, offset],
            recv_sem=back_recv.at[i, offset],
            device_id={"ep": source},
            device_id_type=MESH,
        )

    out_chunk = min(512, out_width)
    for i in range(n_kv):
        down_copies[i].wait()

        def step(n, carry, i=i):
            cols = aligned(n, out_chunk)
            back_out[i, :, cols] = dot(hidden[...], down_w[i, :, cols]).astype(BF16)
            return carry

        lax.fori_loop(0, out_width // out_chunk, step, 0)
        back_in[i, aligned(ep, CAP)] = back_out[i, aligned(ep, CAP)]
        each_peer(lambda offset, i=i: back_copy(i, offset).start())

    for offset in range(1, n_kv):
        final_landing(offset).wait_recv()
    span = lanes * HD // new
    stores = [
        pltpu.make_async_copy(
            final.at[k], attn_hbm.at[:, pl.ds(k * span, span)], store_sem.at[k]
        )
        for k in range(n_kv)
    ]
    for store in stores:
        store.start()

    def part_copy(i):
        return pltpu.make_async_remote_copy(
            src_ref=part_out.at[i],
            dst_ref=part_in.at[i],
            send_sem=part_send.at[i],
            recv_sem=part_recv.at[i],
            device_id={"kv": kv_peer(i + 1)},
            device_id_type=MESH,
        )

    for i in range(n_kv):
        each_peer(lambda offset, i=i: back_landing(i, offset).wait_recv())
        mixed = dot(weights[...], back_in[i], ((0,), (0,)))
        mixed = mixed[:tok_rows] + mixed[tok_rows:]
        if i < n_kv - 1:
            part_out[i] = mixed.astype(BF16)
            part_copy(i).start()
        else:
            own_part[...] = mixed

    result = own_part[...]
    for i in range(n_kv - 1):
        part_copy(i).wait_recv()
        result = result + part_in[i].astype(F32)
    moe_ref[...] = result.astype(BF16)

    for store in stores:
        store.wait()
    for c in range(K_CHUNKS):
        each_peer(lambda offset, c=c: row_copy(c, offset).wait_send())
    for i in range(n_kv):
        each_peer(lambda offset, i=i: back_copy(i, offset).wait_send())
    for i in range(n_kv - 1):
        part_copy(i).wait_send()
    for offset in range(1, n_kv):
        for copy in blend_copies(offset):
            copy.wait_send()
        final_copy(offset).wait_send()


def on_device(
    queries,
    new_keys,
    new_values,
    cache_keys,
    cache_values,
    page_table,
    cached_len,
    moe_rows,
    expert_ids,
    gate_probs,
    w_gate,
    w_up,
    w_down,
):
    n_kv = lax.axis_size("kv")
    n_ep = lax.axis_size("ep")
    new = queries.shape[1]
    tok_rows, width = moe_rows.shape
    units = w_gate.shape[2]
    out_width = width // n_kv
    slots = n_ep * CAP
    depth = width // K_CHUNKS
    lanes = HQ * new // n_kv

    half = HD // 2
    frequency = jnp.power(ROPE_BASE, -2.0 * jnp.arange(half, dtype=F32) / HD)
    positions = cached_len[0] + jnp.arange(new, dtype=jnp.int32)
    angles = positions.astype(F32)[:, None] * frequency[None, :]
    cosine = jnp.cos(angles)
    sine = jnp.sin(angles)

    keys = cache_keys.reshape(-1, KVH * HD)
    vmem = pl.BlockSpec(memory_space=pltpu.VMEM)
    smem = pl.BlockSpec(memory_space=pltpu.SMEM)
    hbm = pl.BlockSpec(memory_space=pl.ANY)
    dma = pltpu.SemaphoreType.DMA
    attn_out, moe_out = pl.pallas_call(
        functools.partial(kernel, n_kv, n_ep),
        out_shape=(
            jax.ShapeDtypeStruct((new, HQ * HD), BF16),
            jax.ShapeDtypeStruct((tok_rows, out_width), BF16),
        ),
        in_specs=[smem, smem] + [hbm] * 5 + [vmem] * 5 + [hbm] * 3,
        out_specs=(hbm, vmem),
        scratch_shapes=[
            pltpu.VMEM((new, HQ * HD), BF16),
            pltpu.VMEM((new, KVH * HD), BF16),
            pltpu.VMEM((new, KVH * HD), BF16),
            pltpu.VMEM(keys.shape, BF16),
            pltpu.VMEM(keys.shape, BF16),
            pltpu.VMEM((width, units), BF16),
            pltpu.VMEM((width, units), BF16),
            pltpu.VMEM((n_kv, units, out_width), BF16),
            pltpu.VMEM((K_CHUNKS, slots, depth), BF16),
            pltpu.VMEM((K_CHUNKS, slots, depth), BF16),
            pltpu.VMEM((slots, units), F32),
            pltpu.VMEM((slots, units), F32),
            pltpu.VMEM((slots, units), BF16),
            pltpu.VMEM((n_kv, slots, out_width), BF16),
            pltpu.VMEM((n_kv, slots, out_width), BF16),
            pltpu.VMEM((n_kv - 1, tok_rows, out_width), BF16),
            pltpu.VMEM((n_kv - 1, tok_rows, out_width), BF16),
            pltpu.VMEM((tok_rows, out_width), F32),
            pltpu.VMEM((slots, 2 * tok_rows), BF16),
            pltpu.VMEM((n_kv, HD, lanes), BF16),
            pltpu.VMEM((n_kv, HD, lanes), BF16),
            pltpu.VMEM((n_kv, 8, lanes), F32),
            pltpu.VMEM((n_kv, 8, lanes), F32),
            pltpu.VMEM((n_kv, new, HQ * HD // n_kv), BF16),
            dma((5,)),
            dma((n_kv,)),
            dma((K_CHUNKS,)),
            dma((K_CHUNKS,)),
            dma((n_kv,)),
            dma((K_CHUNKS, n_ep)),
            dma((K_CHUNKS, n_ep)),
            dma((n_kv, n_ep)),
            dma((n_kv, n_ep)),
            dma((n_kv,)),
            dma((n_kv,)),
            dma((n_kv,)),
            dma((n_kv,)),
            dma((n_kv,)),
            dma((n_kv,)),
            dma((n_kv,)),
            dma((n_kv,)),
        ],
        compiler_params=pltpu.CompilerParams(
            collective_id=0, has_side_effects=True, vmem_limit_bytes=60 * 1024 * 1024
        ),
    )(
        cached_len,
        page_table,
        queries[0],
        new_keys[0],
        new_values[0],
        keys,
        cache_values.reshape(-1, KVH * HD),
        cosine,
        sine,
        moe_rows,
        expert_ids.T,
        gate_probs.T,
        w_gate[0],
        w_up[0],
        w_down[0],
    )
    return attn_out[None], moe_out


def solution(mesh):
    return jax.shard_map(
        on_device,
        mesh=mesh,
        in_specs=(
            P("ep", None, None),
            P("ep", None, None),
            P("ep", None, None),
            P("ep", "kv", None, None),
            P("ep", "kv", None, None),
            P("ep", None),
            P("ep"),
            P("ep", None),
            P("ep", None),
            P("ep", None),
            P("ep", None, "kv"),
            P("ep", None, "kv"),
            P("ep", "kv", None),
        ),
        out_specs=(P("ep", None, None), P("ep", "kv")),
        check_vma=False,
    )
```
